32 devices in a mesh: groups: 2 (over x), tensor: 8 (over z, y), expert: 2 (over core).
Axes of the slice: x: 2, y: 2, z: 4, core: 2. Of those that a mesh axis runs over, the one named last changes fastest.
Arguments:
- tokens: bfloat16 [1024, 6144], P(('groups', 'tensor', 'expert')), parts along dimension 0, may hold values from -6 to 6
- expert_ids: int32 [1024, 2], P(('groups', 'tensor', 'expert')), parts along dimension 0, may hold values from 0 to 7, as said below
- gates: float32 [1024, 2], P(('groups', 'tensor', 'expert')), parts along dimension 0, may hold values from 0.1 to 0.9
- w_gate: bfloat16 [2, 6144, 8192], P('expert', None, 'tensor'), may hold values from -0.078125 to 0.078125
- w_up: bfloat16 [2, 6144, 8192], P('expert', None, 'tensor'), may hold values from -0.078125 to 0.078125
- w_down: bfloat16 [2, 8192, 6144], P('expert', 'tensor'), may hold values from -0.0625 to 0.0625
Outputs:
- layer_out: bfloat16 [1024, 6144], P(('groups', 'tensor', 'expert')), parts along dimension 0
The draws below stay inside these ranges and needn't reach their ends.
There are 2 independent parts, one for each index of `groups`. The reference program is written for one: setup_inputs(seed, part) draws one part's arguments, and reference() takes and returns one part's arrays. A program takes and returns all parts, laid end to end along the dimension named above; an argument that names none is the same for every part. Nothing has to cross between parts.
Inputs may be any that keep to these rules, and one draw needn't show every extreme that they name: `expert_ids`: the 2 ids of a token differ. Among the 32 tokens of one device, each of the experts 0 to 1 is picked by at most 8 tokens, and in every draw one of them is picked by exactly 8 tokens on every device.
All inputs are finite; a program needn't handle non-finite values.
Results may differ from the reference program's by a relative error of at most 0.013.
Values may be sent and summed in bfloat16 or wider, within the bound.
No kernel may reach another device: no remote copies, remote signals or barrier semaphores. Data moves between devices by JAX's collectives and lax.ppermute only.
A program may use at most 128 MiB of HBM per device.

```python
import jax
import jax.numpy as jnp
from jax import lax

D = 6144
EXPERTS_ALL = 8
TOP = 2
FF = 8192
TOK_DEV = 32
CAP = 8
EXPERTS = 2
TOKENS = 512
N_TENSOR = 8


def draw_expert_ids(key, part):
    key = jax.random.fold_in(key, 11)
    subkeys = jax.random.split(key, 6)
    blocks = TOKENS // TOK_DEV
    hot_expert = jax.random.randint(subkeys[0], (), 0, 2)
    cold_loads = jax.random.randint(subkeys[1], (blocks, 2), 1, CAP // 2 + 1)
    loads = jnp.where(jnp.arange(2, dtype=jnp.int32) == hot_expert, CAP, cold_loads)
    scores = jax.random.randint(subkeys[2], (blocks, 2, TOK_DEV), 0, 65536) * TOK_DEV + jnp.arange(TOK_DEV, dtype=jnp.int32)
    ordering = jnp.argsort(scores, axis=-1)
    ranking = jnp.argsort(ordering, axis=-1)
    member = ranking < loads[..., None]
    member_zero = member[:, 0, :]
    member_one = member[:, 1, :]
    others = EXPERTS_ALL - 2
    spare_one = 2 + jax.random.randint(subkeys[3], (blocks, TOK_DEV), 0, others)
    spare_two = 2 + (spare_one - 2 + jax.random.randint(subkeys[4], (blocks, TOK_DEV), 1, others)) % others
    first = jnp.where(member_zero, 0, jnp.where(member_one, 1, spare_one))
    second = jnp.where(member_zero & member_one, 1, jnp.where(member_zero | member_one, spare_one, spare_two))
    flipped = jax.random.randint(subkeys[5], (blocks, TOK_DEV), 0, 2) == 1
    column_a = jnp.where(flipped, second, first)
    column_b = jnp.where(flipped, first, second)
    return jnp.stack([column_a, column_b], axis=-1).reshape(TOKENS, 2).astype(jnp.int32)


def block_levels(key, shape, shards, low, top_value):
    loudness = 1.0
    for position, blocks in shards:
        steps = jax.random.uniform(jax.random.fold_in(jax.random.fold_in(key, 6), position), (blocks,), jnp.float32, low / len(shards), top_value / len(shards))
        loudness = loudness * jnp.repeat(jnp.exp(steps), shape[position] // blocks).reshape((-1,) + (1,) * (len(shape) - 1 - position))
    return loudness


def normal_values(stream_key, dims, spread, bound, cuts=(), held_as=jnp.bfloat16):
    values = jax.random.normal(stream_key, dims, jnp.float32) * spread
    if len(cuts) > 0:
        values = block_levels(stream_key, dims, cuts, -0.22, 0.18) * values
    return jnp.clip(values, min=-bound, max=bound).astype(held_as)


def setup_inputs(seed: int = 0, part: int = 0) -> dict:
    key_list = jax.random.split(jax.random.key(seed), 7)
    own_keys = jax.random.split(jax.random.fold_in(key_list[6], part), 7)
    return {
        "tokens": normal_values(own_keys[0], (TOKENS, D), 1.0, 6.0, ((0, 16),)),
        "expert_ids": draw_expert_ids(jax.random.fold_in(jax.random.fold_in(key_list[6], part), 71), part),
        "gates": jnp.clip(0.1 + 0.79999997 * jax.random.uniform(own_keys[2], (TOKENS, TOP), jnp.float32) ** block_levels(own_keys[2], (TOKENS, TOP), ((0, 16),), -0.2, 0.2), 0.1, 0.9),
        "w_gate": normal_values(key_list[3], (EXPERTS, D, FF), D ** -0.5, 0.078125, ((0, 2), (2, 8))),
        "w_up": normal_values(key_list[4], (EXPERTS, D, FF), D ** -0.5, 0.078125, ((0, 2), (2, 8))),
        "w_down": normal_values(key_list[5], (EXPERTS, FF, D), FF ** -0.5, 0.0625, ((0, 2), (1, 8))),
    }


def reference(tokens, expert_ids, gates, w_gate, w_up, w_down):
    blocks = TOKENS // TOK_DEV
    id_blocks = expert_ids.reshape(blocks, TOK_DEV, TOP)
    gate_vals = gates.reshape(blocks, TOK_DEV, TOP)
    experts = jnp.arange(EXPERTS, dtype=jnp.int32)
    matches = id_blocks[..., None] == experts
    picked = jnp.any(matches, axis=2).astype(jnp.int32)
    weight = jnp.sum(jnp.where(matches, gate_vals[..., None], jnp.float32(0.0)), axis=2)
    slot_of = jnp.cumsum(picked, axis=1) - picked
    onehot = ((picked[..., None] == 1) & (slot_of[..., None] == jnp.arange(CAP, dtype=jnp.int32))).astype(jnp.float32)
    grouped = tokens.reshape(blocks, TOK_DEV, D).astype(jnp.float32)
    routed = jnp.einsum("btec,btd->ebcd", onehot, grouped, precision=lax.Precision.HIGHEST).astype(jnp.bfloat16)
    unit_share = FF // N_TENSOR
    outputs = []
    for expert in range(EXPERTS):
        expert_rows = routed[expert].reshape(blocks * CAP, D)
        gate_proj = jnp.dot(expert_rows, w_gate[expert], preferred_element_type=jnp.float32)
        up_proj = jnp.dot(expert_rows, w_up[expert], preferred_element_type=jnp.float32)
        hidden = (jax.nn.silu(gate_proj) * up_proj).astype(jnp.bfloat16)
        hidden_parts = hidden.reshape(blocks * CAP, N_TENSOR, unit_share).transpose(1, 0, 2)
        down_parts = w_down[expert].reshape(N_TENSOR, unit_share, D)

        def accumulate(running, operands):
            term = jnp.dot(operands[0], operands[1], preferred_element_type=jnp.float32).astype(jnp.bfloat16)
            term = lax.optimization_barrier(term)
            return running + term.astype(jnp.float32), None

        running, _ = lax.scan(accumulate, jnp.zeros((blocks * CAP, D), jnp.float32), (hidden_parts, down_parts))
        outputs.append(running.astype(jnp.bfloat16).reshape(blocks, CAP, D))
    expert_out = jnp.stack(outputs, axis=0).astype(jnp.float32)
    coefficient = onehot * weight[..., None]
    layer_out = jnp.einsum("btec,ebcd->btd", coefficient, expert_out, precision=lax.Precision.HIGHEST)
    return layer_out.reshape(TOKENS, D).astype(jnp.bfloat16)
```

```python
import jax
import jax.numpy as jnp
import numpy as np
from jax import lax
from jax.sharding import PartitionSpec as P


def ring_order(mesh):
    count = mesh.shape["tensor"]
    names = list(mesh.axis_names)
    line = np.moveaxis(mesh.devices, names.index("tensor"), 0).reshape(count, -1)[:, 0]
    natural = list(range(count))
    places = [tuple(getattr(device, "coords", ()) or ()) for device in line]
    if not all(len(place) == 3 for place in places):
        return natural
    varying = [d for d in range(3) if len({place[d] for place in places}) > 1]
    if len(varying) != 2:
        return natural
    inner = [d for d in varying if len({place[d] for place in places}) == 2]
    if not inner:
        return natural
    side = inner[-1]
    along = varying[0] if varying[1] == side else varying[1]
    low = min(place[side] for place in places)
    up = sorted((i for i in natural if places[i][side] == low), key=lambda i: places[i][along])
    down = sorted((i for i in natural if places[i][side] != low), key=lambda i: -places[i][along])
    return up + down


def make_per_device(ring):
    count = len(ring)
    forward = [(ring[i], ring[(i + 1) % count]) for i in range(count)]
    backward = [(b, a) for a, b in forward]
    swap = [(0, 1), (1, 0)]
    longer, shorter = count // 2, (count - 1) // 2

    def gather(block, forward_steps, backward_steps):
        held = {0: block}
        ahead = behind = block
        for step in range(1, max(forward_steps, backward_steps) + 1):
            if step <= forward_steps:
                behind = lax.ppermute(behind, "tensor", forward)
                held[-step] = behind
            if step <= backward_steps:
                ahead = lax.ppermute(ahead, "tensor", backward)
                held[step] = ahead
        return held

    def scatter_sum(terms, forward_steps, backward_steps):
        def flow(steps, sign, perm):
            running = None
            for step in range(steps, 0, -1):
                distance = sign * step
                term = terms[distance] if distance in terms else terms[distance - sign * count]
                total = term if running is None else term + running.astype(jnp.float32)
                running = lax.ppermute(total.astype(jnp.bfloat16), "tensor", perm)
            return running

        total = terms[0]
        for part in (flow(forward_steps, 1, forward), flow(backward_steps, -1, backward)):
            if part is not None:
                total = total + part.astype(jnp.float32)
        return total

    def per_device(tokens, expert_ids, gates, w_gate, w_up, w_down):
        expert_count = lax.axis_size("expert")
        rows_here = tokens.shape[0]
        capacity = rows_here // 4
        own = lax.axis_index("expert")
        experts = (own + jnp.arange(expert_count, dtype=jnp.int32)) % expert_count
        matches = expert_ids[:, :, None] == experts
        picked = jnp.any(matches, axis=1).astype(jnp.int32)
        weight = jnp.sum(jnp.where(matches, gates[:, :, None], jnp.float32(0.0)), axis=1)
        slot_of = jnp.cumsum(picked, axis=0) - picked
        onehot = (
            (picked[..., None] == 1) & (slot_of[..., None] == jnp.arange(capacity, dtype=jnp.int32))
        ).astype(jnp.bfloat16)
        routed = jnp.einsum("tec,td->ecd", onehot, tokens, preferred_element_type=jnp.float32).astype(
            jnp.bfloat16
        )
        sibling = lax.ppermute(routed[1], "expert", swap)
        held_a = gather(routed[0], longer, shorter)
        held_b = gather(sibling, shorter, longer)
        keys = [("a", k) for k in held_a] + [("b", k) for k in held_b]
        rows = jnp.concatenate(list(held_a.values()) + list(held_b.values()), axis=0)
        gate_proj = jnp.dot(rows, w_gate[0], preferred_element_type=jnp.float32)
        up_proj = jnp.dot(rows, w_up[0], preferred_element_type=jnp.float32)
        hidden = (jax.nn.silu(gate_proj) * up_proj).astype(jnp.bfloat16)
        parts = jnp.dot(hidden, w_down[0], preferred_element_type=jnp.float32)
        terms = {"a": {}, "b": {}}
        for i, (chain, distance) in enumerate(keys):
            terms[chain][distance] = parts[i * capacity : (i + 1) * capacity]
        sum_b = scatter_sum(terms["b"], shorter, longer)
        other = lax.ppermute(sum_b.astype(jnp.bfloat16), "expert", swap)
        sum_a = scatter_sum(terms["a"], longer, shorter).astype(jnp.bfloat16)
        returned = jnp.stack([sum_a, other]).astype(jnp.float32)
        coefficient = onehot.astype(jnp.float32) * weight[:, :, None]
        layer_out = jnp.einsum(
            "tec,ecd->td", coefficient, returned, precision=lax.Precision.HIGHEST
        )
        return layer_out.astype(jnp.bfloat16)

    return per_device


def solution(mesh):
    placed = (
        P(("groups", "tensor", "expert"), None),
        P(("groups", "tensor", "expert"), None),
        P(("groups", "tensor", "expert"), None),
        P("expert", None, "tensor"),
        P("expert", None, "tensor"),
        P("expert", "tensor", None),
    )
    return jax.shard_map(
        make_per_device(ring_order(mesh)),
        mesh=mesh,
        in_specs=placed,
        out_specs=P(("groups", "tensor", "expert"), None),
        check_vma=False,
    )
```

```python
import functools

import jax
import jax.numpy as jnp
import numpy as np
from jax import lax
from jax.experimental import pallas as pl
from jax.experimental.pallas import tpu as pltpu
from jax.sharding import PartitionSpec as P


def ring_order(mesh):
    count = mesh.shape["tensor"]
    names = list(mesh.axis_names)
    line = np.moveaxis(mesh.devices, names.index("tensor"), 0).reshape(count, -1)[:, 0]
    natural = list(range(count))
    places = [tuple(getattr(device, "coords", ()) or ()) for device in line]
    if not all(len(place) == 3 for place in places):
        return natural
    varying = [d for d in range(3) if len({place[d] for place in places}) > 1]
    if len(varying) != 2:
        return natural
    inner = [d for d in varying if len({place[d] for place in places}) == 2]
    if not inner:
        return natural
    side = inner[-1]
    along = varying[0] if varying[1] == side else varying[1]
    low = min(place[side] for place in places)
    up = sorted((i for i in natural if places[i][side] == low), key=lambda i: places[i][along])
    down = sorted((i for i in natural if places[i][side] != low), key=lambda i: -places[i][along])
    return up + down


def route_kernel(own, ids, gates, tokens, mine, theirs, coefficient):
    rows_here = tokens.shape[0]
    capacity = mine.shape[0]
    earlier = (
        lax.broadcasted_iota(jnp.int32, (rows_here, rows_here), 0)
        < lax.broadcasted_iota(jnp.int32, (rows_here, rows_here), 1)
    ).astype(jnp.float32)
    slots = lax.broadcasted_iota(jnp.int32, (capacity, rows_here), 0).astype(jnp.float32)
    for side, rows in enumerate((mine, theirs)):
        expert = own[0] if side == 0 else 1 - own[0]
        matches = ids[...] == expert
        picked = jnp.sum(matches.astype(jnp.float32), axis=0, keepdims=True)
        weight = jnp.sum(jnp.where(matches, gates[...], 0.0), axis=0, keepdims=True)
        slot = jnp.dot(
            jnp.broadcast_to(picked, (capacity, rows_here)), earlier, preferred_element_type=jnp.float32
        )
        onehot = jnp.where((picked > 0.0) & (slot == slots), 1.0, 0.0)
        rows[...] = jnp.dot(
            onehot.astype(jnp.bfloat16), tokens[...], preferred_element_type=jnp.float32
        ).astype(rows.dtype)
        coefficient[side * capacity : (side + 1) * capacity, :] = onehot * weight


def route(own, ids, gates, tokens):
    rows_here, width = tokens.shape
    capacity = rows_here // 4
    in_vmem = pl.BlockSpec(memory_space=pltpu.VMEM)
    return pl.pallas_call(
        route_kernel,
        out_shape=[
            pltpu.VMEM((capacity, width), tokens.dtype),
            pltpu.VMEM((capacity, width), tokens.dtype),
            pltpu.VMEM((2 * capacity, rows_here), jnp.float32),
        ],
        in_specs=[pl.BlockSpec(memory_space=pltpu.SMEM), in_vmem, in_vmem, in_vmem],
        out_specs=[in_vmem] * 3,
        compiler_params=pltpu.CompilerParams(vmem_limit_bytes=4 * 1024 * 1024),
        cost_estimate=pl.CostEstimate(flops=30_000_000_000, bytes_accessed=0, transcendentals=0),
    )(own, ids, gates, tokens)


def combine_kernel(coefficient, first, second, out):
    left = coefficient[...]
    high = left.astype(jnp.bfloat16)
    rest = left - high.astype(jnp.float32)
    middle = rest.astype(jnp.bfloat16)
    low = (rest - middle.astype(jnp.float32)).astype(jnp.bfloat16)
    split = jnp.concatenate([high, middle, low], axis=0)
    pair = jnp.concatenate([first[...], second[...]], axis=0)
    rows = jnp.concatenate([pair, pair, pair], axis=0)
    out[...] = lax.dot_general(
        split, rows, (((0,), (0,)), ((), ())), preferred_element_type=jnp.float32
    ).astype(out.dtype)


def combine(coefficient, first, second):
    rows_here, width = coefficient.shape[1], first.shape[1]
    in_vmem = pl.BlockSpec(memory_space=pltpu.VMEM)
    return pl.pallas_call(
        combine_kernel,
        out_shape=jax.ShapeDtypeStruct((rows_here, width), first.dtype),
        in_specs=[in_vmem] * 3,
        out_specs=in_vmem,
        compiler_params=pltpu.CompilerParams(vmem_limit_bytes=4 * 1024 * 1024),
    )(coefficient, first, second)


def feed_forward_kernel(count, capacity, *refs):
    blocks, (w_gate, w_up, w_down) = refs[:count], refs[count : count + 3]
    outs = refs[count + 3 : 2 * count + 3]
    rows, hidden = refs[2 * count + 3 :]
    for i, block in enumerate(blocks):
        rows[i * capacity : (i + 1) * capacity, :] = block[...]
    units, width = w_down.shape
    step = min(256, units)

    @pl.loop(0, units // step)
    def _(j):
        here = pl.ds(pl.multiple_of(j * step, step), step)
        gate = jnp.dot(rows[...], w_gate[:, here], preferred_element_type=jnp.float32)
        up = jnp.dot(rows[...], w_up[:, here], preferred_element_type=jnp.float32)
        hidden[:, here] = (gate / (1.0 + jnp.exp(-gate)) * up).astype(hidden.dtype)

    @pl.loop(0, width // 512)
    def _(j):
        here = pl.ds(pl.multiple_of(j * 512, 512), 512)
        part = jnp.dot(hidden[...], w_down[:, here], preferred_element_type=jnp.float32)
        for i, out in enumerate(outs):
            out[:, here] = part[i * capacity : (i + 1) * capacity]


def feed_forward(blocks, w_gate, w_up, w_down):
    count, (capacity, width) = len(blocks), blocks[0].shape
    units = w_down.shape[0]
    weights = [pltpu.with_memory_space_constraint(w, pltpu.VMEM) for w in (w_gate, w_up, w_down)]
    in_vmem = pl.BlockSpec(memory_space=pltpu.VMEM)
    return pl.pallas_call(
        functools.partial(feed_forward_kernel, count, capacity),
        out_shape=[pltpu.VMEM((capacity, width), jnp.float32) for _ in blocks],
        in_specs=[in_vmem] * (count + 3),
        out_specs=[in_vmem] * count,
        scratch_shapes=[
            pltpu.VMEM((count * capacity, width), jnp.bfloat16),
            pltpu.VMEM((count * capacity, units), jnp.bfloat16),
        ],
        compiler_params=pltpu.CompilerParams(vmem_limit_bytes=12 * 1024 * 1024),
        cost_estimate=pl.CostEstimate(
            flops=6 * count * capacity * width * units, bytes_accessed=0, transcendentals=0
        ),
    )(*[pltpu.with_memory_space_constraint(b, pltpu.VMEM) for b in blocks], *weights)


def make_per_device(ring):
    count = len(ring)
    forward = [(ring[i], ring[(i + 1) % count]) for i in range(count)]
    backward = [(b, a) for a, b in forward]
    swap = [(0, 1), (1, 0)]
    longer, shorter = count // 2, (count - 1) // 2

    def gather(block, forward_steps, backward_steps):
        held = {0: block}
        ahead = behind = block
        for step in range(1, max(forward_steps, backward_steps) + 1):
            if step <= forward_steps:
                behind = lax.ppermute(behind, "tensor", forward)
                held[-step] = behind
            if step <= backward_steps:
                ahead = lax.ppermute(ahead, "tensor", backward)
                held[step] = ahead
        return held

    def scatter_sum(terms, forward_steps, backward_steps):
        def flow(steps, sign, perm):
            running = None
            for step in range(steps, 0, -1):
                distance = sign * step
                term = terms[distance] if distance in terms else terms[distance - sign * count]
                total = term if running is None else term + running.astype(jnp.float32)
                running = lax.ppermute(total.astype(jnp.bfloat16), "tensor", perm)
            return running

        total = terms[0]
        for part in (flow(forward_steps, 1, forward), flow(backward_steps, -1, backward)):
            if part is not None:
                total = total + part.astype(jnp.float32)
        return total

    def per_device(tokens, expert_ids, gates, w_gate, w_up, w_down):
        own = lax.axis_index("expert").astype(jnp.int32).reshape(1)
        mine, theirs, coefficient = route(own, expert_ids.T, gates.T, tokens)
        sibling = lax.ppermute(theirs, "expert", swap)
        held_a = gather(mine, longer, shorter)
        held_b = gather(sibling, shorter, longer)
        keys = [("a", k) for k in held_a] + [("b", k) for k in held_b]
        blocks = list(held_a.values()) + list(held_b.values())
        parts = feed_forward(blocks, w_gate[0], w_up[0], w_down[0])
        terms = {"a": {}, "b": {}}
        for (chain, distance), part in zip(keys, parts):
            terms[chain][distance] = part
        sum_b = scatter_sum(terms["b"], shorter, longer)
        other = lax.ppermute(sum_b.astype(jnp.bfloat16), "expert", swap)
        sum_a = scatter_sum(terms["a"], longer, shorter).astype(jnp.bfloat16)
        return combine(coefficient, sum_a, other)

    return per_device


def solution(mesh):
    placed = (
        P(("groups", "tensor", "expert"), None),
        P(("groups", "tensor", "expert"), None),
        P(("groups", "tensor", "expert"), None),
        P("expert", None, "tensor"),
        P("expert", None, "tensor"),
        P("expert", "tensor", None),
    )
    return jax.shard_map(
        make_per_device(ring_order(mesh)),
        mesh=mesh,
        in_specs=placed,
        out_specs=P(("groups", "tensor", "expert"), None),
        check_vma=False,
    )
```

```python
import functools

import jax
import jax.numpy as jnp
import numpy as np
from jax import lax
from jax.experimental import pallas as pl
from jax.experimental.pallas import tpu as pltpu
from jax.sharding import PartitionSpec as P


def ring_order(mesh):
    count = mesh.shape["tensor"]
    names = list(mesh.axis_names)
    line = np.moveaxis(mesh.devices, names.index("tensor"), 0).reshape(count, -1)[:, 0]
    natural = list(range(count))
    places = [tuple(getattr(device, "coords", ()) or ()) for device in line]
    if not all(len(place) == 3 for place in places):
        return natural
    varying = [d for d in range(3) if len({place[d] for place in places}) > 1]
    if len(varying) != 2:
        return natural
    inner = [d for d in varying if len({place[d] for place in places}) == 2]
    if not inner:
        return natural
    side = inner[-1]
    along = varying[0] if varying[1] == side else varying[1]
    low = min(place[side] for place in places)
    up = sorted((i for i in natural if places[i][side] == low), key=lambda i: places[i][along])
    down = sorted((i for i in natural if places[i][side] != low), key=lambda i: -places[i][along])
    return up + down


def route_kernel(own, *refs):
    sources, (mine, theirs, coefficient) = refs[:3], refs[3:6]
    (ids, gates, tokens), arrived = refs[6:9], refs[9]
    copies = [
        pltpu.make_async_copy(source, target, arrived.at[i])
        for i, (source, target) in enumerate(zip(sources, (ids, gates, tokens)))
    ]
    for copy in copies:
        copy.start()
    for copy in copies:
        copy.wait()
    rows_here = tokens.shape[0]
    capacity = mine.shape[0]
    earlier = (
        lax.broadcasted_iota(jnp.int32, (rows_here, rows_here), 0)
        < lax.broadcasted_iota(jnp.int32, (rows_here, rows_here), 1)
    ).astype(jnp.float32)
    slots = lax.broadcasted_iota(jnp.int32, (capacity, rows_here), 0).astype(jnp.float32)
    for side, rows in enumerate((mine, theirs)):
        expert = own[0] if side == 0 else 1 - own[0]
        matches = ids[...] == expert
        picked = jnp.sum(matches.astype(jnp.float32), axis=0, keepdims=True)
        weight = jnp.sum(jnp.where(matches, gates[...], 0.0), axis=0, keepdims=True)
        slot = jnp.dot(
            jnp.broadcast_to(picked, (capacity, rows_here)), earlier, preferred_element_type=jnp.float32
        )
        onehot = jnp.where((picked > 0.0) & (slot == slots), 1.0, 0.0)
        rows[...] = jnp.dot(
            onehot.astype(jnp.bfloat16), tokens[...], preferred_element_type=jnp.float32
        ).astype(rows.dtype)
        coefficient[side * capacity : (side + 1) * capacity, :] = onehot * weight


def route(own, ids, gates, tokens):
    rows_here, width = tokens.shape
    capacity = rows_here // 4
    in_vmem = pl.BlockSpec(memory_space=pltpu.VMEM)
    return pl.pallas_call(
        route_kernel,
        out_shape=[
            pltpu.VMEM((capacity, width), tokens.dtype),
            pltpu.VMEM((capacity, width), tokens.dtype),
            pltpu.VMEM((2 * capacity, rows_here), jnp.float32),
        ],
        in_specs=[pl.BlockSpec(memory_space=pltpu.SMEM)] + [pl.BlockSpec(memory_space=pl.ANY)] * 3,
        out_specs=[in_vmem] * 3,
        scratch_shapes=[pltpu.VMEM(a.shape, a.dtype) for a in (ids, gates, tokens)]
        + [pltpu.SemaphoreType.DMA((3,))],
        compiler_params=pltpu.CompilerParams(vmem_limit_bytes=4 * 1024 * 1024),
        cost_estimate=pl.CostEstimate(flops=30_000_000_000, bytes_accessed=0, transcendentals=0),
    )(own, *[pltpu.with_memory_space_constraint(a, pltpu.HBM) for a in (ids, gates, tokens)])


def combine_kernel(coefficient, first, second, out):
    left = coefficient[...]
    high = left.astype(jnp.bfloat16)
    rest = left - high.astype(jnp.float32)
    middle = rest.astype(jnp.bfloat16)
    low = (rest - middle.astype(jnp.float32)).astype(jnp.bfloat16)
    split = jnp.concatenate([high, middle, low], axis=0)
    pair = jnp.concatenate([first[...], second[...]], axis=0)
    rows = jnp.concatenate([pair, pair, pair], axis=0)
    out[...] = lax.dot_general(
        split, rows, (((0,), (0,)), ((), ())), preferred_element_type=jnp.float32
    ).astype(out.dtype)


def combine(coefficient, first, second):
    rows_here, width = coefficient.shape[1], first.shape[1]
    in_vmem = pl.BlockSpec(memory_space=pltpu.VMEM)
    return pl.pallas_call(
        combine_kernel,
        out_shape=jax.ShapeDtypeStruct((rows_here, width), first.dtype),
        in_specs=[in_vmem] * 3,
        out_specs=in_vmem,
        compiler_params=pltpu.CompilerParams(vmem_limit_bytes=4 * 1024 * 1024),
    )(coefficient, first, second)


def feed_forward_kernel(count, capacity, *refs):
    blocks, (w_gate, w_up, w_down) = refs[:count], refs[count : count + 3]
    outs = refs[count + 3 : 2 * count + 3]
    rows, gate, hidden, parts = refs[2 * count + 3 :]
    for i, block in enumerate(blocks):
        rows[i * capacity : (i + 1) * capacity, :] = block[...]
    gate[...] = jnp.dot(rows[...], w_gate[...], preferred_element_type=jnp.float32)
    up = jnp.dot(rows[...], w_up[...], preferred_element_type=jnp.float32)
    hidden[...] = (gate[...] / (1.0 + jnp.exp(-gate[...])) * up).astype(hidden.dtype)
    parts[...] = jnp.dot(hidden[...], w_down[...], preferred_element_type=jnp.float32).astype(parts.dtype)
    for i, out in enumerate(outs):
        out[...] = parts[i * capacity : (i + 1) * capacity, :].astype(out.dtype)


def feed_forward(blocks, w_gate, w_up, w_down):
    count, (capacity, width) = len(blocks), blocks[0].shape
    units = w_down.shape[0]
    weights = [pltpu.with_memory_space_constraint(w, pltpu.VMEM) for w in (w_gate, w_up, w_down)]
    in_vmem = pl.BlockSpec(memory_space=pltpu.VMEM)
    parts = pl.pallas_call(
        functools.partial(feed_forward_kernel, count, capacity),
        out_shape=[pltpu.VMEM((capacity, width), jnp.float32) for _ in blocks],
        in_specs=[in_vmem] * (count + 3),
        out_specs=[in_vmem] * count,
        scratch_shapes=[
            pltpu.VMEM((count * capacity, width), jnp.bfloat16),
            pltpu.VMEM((count * capacity, units), jnp.float32),
            pltpu.VMEM((count * capacity, units), jnp.bfloat16),
            pltpu.VMEM((count * capacity, width), jnp.float32),
        ],
        compiler_params=pltpu.CompilerParams(vmem_limit_bytes=12 * 1024 * 1024),
        cost_estimate=pl.CostEstimate(
            flops=6 * count * capacity * width * units, bytes_accessed=0, transcendentals=0
        ),
    )(*[pltpu.with_memory_space_constraint(b, pltpu.VMEM) for b in blocks], *weights)
    return parts


def make_per_device(ring):
    count = len(ring)
    forward = [(ring[i], ring[(i + 1) % count]) for i in range(count)]
    backward = [(b, a) for a, b in forward]
    swap = [(0, 1), (1, 0)]
    longer, shorter = count // 2, (count - 1) // 2

    def gather(block, forward_steps, backward_steps):
        held = {0: block}
        ahead = behind = block
        for step in range(1, max(forward_steps, backward_steps) + 1):
            if step <= forward_steps:
                behind = lax.ppermute(behind, "tensor", forward)
                held[-step] = behind
            if step <= backward_steps:
                ahead = lax.ppermute(ahead, "tensor", backward)
                held[step] = ahead
        return held

    def scatter_sum(terms, forward_steps, backward_steps):
        def flow(steps, sign, perm):
            running = None
            for step in range(steps, 0, -1):
                distance = sign * step
                term = terms[distance] if distance in terms else terms[distance - sign * count]
                total = term.astype(jnp.float32) + (0 if running is None else running.astype(jnp.float32))
                running = lax.ppermute(total.astype(jnp.bfloat16), "tensor", perm)
            return running

        total = terms[0].astype(jnp.float32)
        for part in (flow(forward_steps, 1, forward), flow(backward_steps, -1, backward)):
            if part is not None:
                total = total + part.astype(jnp.float32)
        return total

    def per_device(tokens, expert_ids, gates, w_gate, w_up, w_down):
        own = lax.axis_index("expert").astype(jnp.int32).reshape(1)
        mine, theirs, coefficient = route(own, expert_ids.T, gates.T, tokens)
        sibling = lax.ppermute(theirs, "expert", swap)
        held_a = gather(mine, longer, shorter)
        held_b = gather(sibling, shorter, longer)
        keys = [("a", k) for k in held_a] + [("b", k) for k in held_b]
        blocks = list(held_a.values()) + list(held_b.values())
        parts = feed_forward(blocks, w_gate[0], w_up[0], w_down[0])
        terms = {"a": {}, "b": {}}
        for (chain, distance), part in zip(keys, parts):
            terms[chain][distance] = part
        sum_b = scatter_sum(terms["b"], shorter, longer)
        other = lax.ppermute(sum_b.astype(jnp.bfloat16), "expert", swap)
        sum_a = scatter_sum(terms["a"], longer, shorter).astype(jnp.bfloat16)
        return combine(coefficient, sum_a, other)

    return per_device


def solution(mesh):
    placed = (
        P(("groups", "tensor", "expert"), None),
        P(("groups", "tensor", "expert"), None),
        P(("groups", "tensor", "expert"), None),
        P("expert", None, "tensor"),
        P("expert", None, "tensor"),
        P("expert", "tensor", None),
    )
    return jax.shard_map(
        make_per_device(ring_order(mesh)),
        mesh=mesh,
        in_specs=placed,
        out_specs=P(("groups", "tensor", "expert"), None),
        check_vma=False,
    )
```

```python
import functools

import jax
import jax.numpy as jnp
import numpy as np
from jax import lax
from jax.experimental import pallas as pl
from jax.experimental.pallas import tpu as pltpu
from jax.sharding import PartitionSpec as P


def ring_order(mesh):
    count = mesh.shape["tensor"]
    names = list(mesh.axis_names)
    line = np.moveaxis(mesh.devices, names.index("tensor"), 0).reshape(count, -1)[:, 0]
    natural = list(range(count))
    places = [tuple(getattr(device, "coords", ()) or ()) for device in line]
    if not all(len(place) == 3 for place in places):
        return natural
    varying = [d for d in range(3) if len({place[d] for place in places}) > 1]
    if len(varying) != 2:
        return natural
    inner = [d for d in varying if len({place[d] for place in places}) == 2]
    if not inner:
        return natural
    side = inner[-1]
    along = varying[0] if varying[1] == side else varying[1]
    low = min(place[side] for place in places)
    up = sorted((i for i in natural if places[i][side] == low), key=lambda i: places[i][along])
    down = sorted((i for i in natural if places[i][side] != low), key=lambda i: -places[i][along])
    return up + down


def route_kernel(own, *refs):
    sources, (mine, theirs, coefficient) = refs[:3], refs[3:6]
    (ids, gates, tokens), arrived = refs[6:9], refs[9]
    copies = [
        pltpu.make_async_copy(source, target, arrived.at[i])
        for i, (source, target) in enumerate(zip(sources, (ids, gates, tokens)))
    ]
    for copy in copies:
        copy.start()
    for copy in copies:
        copy.wait()
    rows_here, capacity = tokens.shape[0], mine.shape[0]
    place = lax.broadcasted_iota(jnp.int32, (2 * capacity, rows_here), 0)
    expert = jnp.where(place < capacity, own[0], 1 - own[0])
    slots = jnp.where(place < capacity, place, place - capacity).astype(jnp.float32)
    earlier = lax.broadcasted_iota(jnp.int32, (rows_here, rows_here), 0) < lax.broadcasted_iota(
        jnp.int32, (rows_here, rows_here), 1
    )
    matches = [ids[k : k + 1, :] == expert for k in range(ids.shape[0])]
    picked = functools.reduce(jnp.logical_or, matches)
    weight = sum(jnp.where(match, gates[k : k + 1, :], 0.0) for k, match in enumerate(matches))
    slot = jnp.dot(
        picked.astype(jnp.float32).astype(jnp.bfloat16),
        earlier.astype(jnp.float32).astype(jnp.bfloat16),
        preferred_element_type=jnp.float32,
    )
    onehot = jnp.where(picked & (slot == slots), 1.0, 0.0)
    rows = jnp.dot(onehot.astype(jnp.bfloat16), tokens[...], preferred_element_type=jnp.float32)
    mine[...] = rows[:capacity].astype(mine.dtype)
    theirs[...] = rows[capacity:].astype(theirs.dtype)
    coefficient[...] = onehot * weight


def route(own, ids, gates, tokens):
    rows_here, width = tokens.shape
    capacity = rows_here // 4
    in_vmem = pl.BlockSpec(memory_space=pltpu.VMEM)
    return pl.pallas_call(
        route_kernel,
        out_shape=[
            pltpu.VMEM((capacity, width), tokens.dtype),
            pltpu.VMEM((capacity, width), tokens.dtype),
            pltpu.VMEM((2 * capacity, rows_here), jnp.float32),
        ],
        in_specs=[pl.BlockSpec(memory_space=pltpu.SMEM)] + [pl.BlockSpec(memory_space=pl.ANY)] * 3,
        out_specs=[in_vmem] * 3,
        scratch_shapes=[pltpu.VMEM(a.shape, a.dtype) for a in (ids, gates, tokens)]
        + [pltpu.SemaphoreType.DMA((3,))],
        compiler_params=pltpu.CompilerParams(vmem_limit_bytes=4 * 1024 * 1024),
        cost_estimate=pl.CostEstimate(flops=30_000_000_000, bytes_accessed=0, transcendentals=0),
    )(own, *[pltpu.with_memory_space_constraint(a, pltpu.HBM) for a in (ids, gates, tokens)])


def presum_kernel(counts, *refs):
    parts, outs = refs[:-2], refs[-2:]
    for group, out in zip((parts[: counts[0]], parts[counts[0] :]), outs):
        total = group[0][...].astype(jnp.float32)
        for part in group[1:]:
            total = total + part[...].astype(jnp.float32)
        out[...] = total


def presum(own, other):
    in_vmem = pl.BlockSpec(memory_space=pltpu.VMEM)
    parts = [pltpu.with_memory_space_constraint(part, pltpu.VMEM) for part in (*own, *other)]
    return pl.pallas_call(
        functools.partial(presum_kernel, (len(own), len(other))),
        out_shape=[pltpu.VMEM(own[0].shape, jnp.float32)] * 2,
        in_specs=[in_vmem] * len(parts),
        out_specs=[in_vmem] * 2,
        compiler_params=pltpu.CompilerParams(vmem_limit_bytes=4 * 1024 * 1024),
        cost_estimate=pl.CostEstimate(flops=4_000_000_000, bytes_accessed=0, transcendentals=0),
    )(*parts)


def combine_kernel(counts, coefficient, *refs):
    (*parts, out) = refs
    left = coefficient[...]
    high = left.astype(jnp.bfloat16)
    rest = left - high.astype(jnp.float32)
    middle = rest.astype(jnp.bfloat16)
    low = (rest - middle.astype(jnp.float32)).astype(jnp.bfloat16)
    split = jnp.concatenate([high, middle, low], axis=0)
    sums = []
    for group in (parts[: counts[0]], parts[counts[0] :]):
        total = group[0][...].astype(jnp.float32)
        for part in group[1:]:
            total = total + part[...].astype(jnp.float32)
        sums.append(total.astype(jnp.bfloat16))
    pair = jnp.concatenate(sums, axis=0)
    rows = jnp.concatenate([pair, pair, pair], axis=0)
    out[...] = lax.dot_general(
        split, rows, (((0,), (0,)), ((), ())), preferred_element_type=jnp.float32
    ).astype(out.dtype)


def combine(coefficient, own, other):
    rows_here, width = coefficient.shape[1], own[0].shape[1]
    in_vmem = pl.BlockSpec(memory_space=pltpu.VMEM)
    parts = [pltpu.with_memory_space_constraint(part, pltpu.VMEM) for part in (*own, *other)]
    return pl.pallas_call(
        functools.partial(combine_kernel, (len(own), len(other))),
        out_shape=jax.ShapeDtypeStruct((rows_here, width), jnp.bfloat16),
        in_specs=[in_vmem] * (1 + len(parts)),
        out_specs=in_vmem,
        compiler_params=pltpu.CompilerParams(vmem_limit_bytes=6 * 1024 * 1024),
    )(coefficient, *parts)


def feed_forward_kernel(count, capacity, *refs):
    blocks, (w_gate, w_up, w_down) = refs[:count], refs[count : count + 3]
    outs = refs[count + 3 : 2 * count + 3]
    rows, gate, hidden, parts = refs[2 * count + 3 :]
    for i, block in enumerate(blocks):
        rows[i * capacity : (i + 1) * capacity, :] = block[...]
    gate[...] = jnp.dot(rows[...], w_gate[...], preferred_element_type=jnp.float32)
    up = jnp.dot(rows[...], w_up[...], preferred_element_type=jnp.float32)
    hidden[...] = (gate[...] / (1.0 + jnp.exp(-gate[...])) * up).astype(hidden.dtype)
    parts[...] = jnp.dot(hidden[...], w_down[...], preferred_element_type=jnp.float32).astype(parts.dtype)
    for i, out in enumerate(outs):
        out[...] = parts[i * capacity : (i + 1) * capacity, :].astype(out.dtype)


def feed_forward(blocks, w_gate, w_up, w_down):
    count, (capacity, width) = len(blocks), blocks[0].shape
    units = w_down.shape[0]
    weights = [pltpu.with_memory_space_constraint(w, pltpu.VMEM) for w in (w_gate, w_up, w_down)]
    in_vmem = pl.BlockSpec(memory_space=pltpu.VMEM)
    parts = pl.pallas_call(
        functools.partial(feed_forward_kernel, count, capacity),
        out_shape=[pltpu.VMEM((capacity, width), jnp.float32) for _ in blocks],
        in_specs=[in_vmem] * (count + 3),
        out_specs=[in_vmem] * count,
        scratch_shapes=[
            pltpu.VMEM((count * capacity, width), jnp.bfloat16),
            pltpu.VMEM((count * capacity, units), jnp.float32),
            pltpu.VMEM((count * capacity, units), jnp.bfloat16),
            pltpu.VMEM((count * capacity, width), jnp.float32),
        ],
        compiler_params=pltpu.CompilerParams(vmem_limit_bytes=12 * 1024 * 1024),
        cost_estimate=pl.CostEstimate(
            flops=6 * count * capacity * width * units, bytes_accessed=0, transcendentals=0
        ),
    )(*[pltpu.with_memory_space_constraint(b, pltpu.VMEM) for b in blocks], *weights)
    return parts


def make_per_device(ring):
    count = len(ring)
    near, opposite = (count - 1) // 2, count // 2
    hop, cross = {}, {}
    for way in (1, -1):
        links = [(ring[i], ring[(i + way) % count]) for i in range(count)]
        hop[way] = [(2 * a + core, 2 * b + core) for a, b in links for core in (0, 1)]
        cross[way] = [(2 * a + core, 2 * b + 1 - core) for a, b in links for core in (0, 1)]
    swap = [(0, 1), (1, 0)]
    steps = [(chain, -way * step, way) for step in range(1, near + 1) for chain in (0, 1) for way in (1, -1)]
    if count % 2 == 0:
        steps += [(0, -opposite, 1), (1, opposite, -1)]

    def send(block, perm):
        return lax.ppermute(block, ("tensor", "expert"), perm)

    def gather(mine, theirs):
        held = ({0: mine}, {0: lax.ppermute(theirs, "expert", swap)})
        for chain, place, way in steps:
            if place + way:
                held[chain][place] = send(held[chain][place + way], hop[way])
            elif chain:
                held[chain][place] = send(theirs, cross[way])
            else:
                held[chain][place] = send(mine, hop[way])
        return held

    def scatter(terms):
        arrived = ({}, {})
        other = lax.ppermute(terms[1][0].astype(jnp.bfloat16), "expert", swap)
        for chain, place, way in reversed(steps):
            place, far = -place, abs(place) == opposite and count % 2 == 0
            term = terms[chain][-place if far else place].astype(jnp.float32)
            parts = arrived[chain].pop(place, ())
            for part in parts:
                term = term + part.astype(jnp.float32)
            term = term.astype(jnp.bfloat16)
            last = place == way
            got = send(term, cross[way] if last and chain else hop[way])
            arrived[chain].setdefault(place - way, []).append(got)
        late = [arrived[chain].get(0, [None])[(-1, 0)[chain]] for chain in (0, 1)]
        soon = [[part for part in arrived[chain].get(0, ()) if part is not late[chain]] for chain in (0, 1)]
        return presum([terms[0][0], *soon[0]], [other, *soon[1]]), late

    def per_device(tokens, expert_ids, gates, w_gate, w_up, w_down):
        own = lax.axis_index("expert").astype(jnp.int32).reshape(1)
        mine, theirs, coefficient = route(own, expert_ids.T, gates.T, tokens)
        held = gather(mine, theirs)
        places = [(chain, place) for chain in (0, 1) for place in held[chain]]
        parts = feed_forward([held[c][p] for c, p in places], w_gate[0], w_up[0], w_down[0])
        terms = ({}, {})
        for (chain, place), part in zip(places, parts):
            terms[chain][place] = part
        (first, second), late = scatter(terms)
        return combine(coefficient, [p for p in (first, late[0]) if p is not None], [p for p in (second, late[1]) if p is not None])

    return per_device


def solution(mesh):
    placed = (
        P(("groups", "tensor", "expert"), None),
        P(("groups", "tensor", "expert"), None),
        P(("groups", "tensor", "expert"), None),
        P("expert", None, "tensor"),
        P("expert", None, "tensor"),
        P("expert", "tensor", None),
    )
    return jax.shard_map(
        make_per_device(ring_order(mesh)),
        mesh=mesh,
        in_specs=placed,
        out_specs=P(("groups", "tensor", "expert"), None),
        check_vma=False,
    )
```

```python
import functools

import jax
import jax.numpy as jnp
import numpy as np
from jax import lax
from jax.experimental import pallas as pl
from jax.experimental.pallas import tpu as pltpu
from jax.sharding import PartitionSpec as P


def ring_order(mesh):
    count = mesh.shape["tensor"]
    names = list(mesh.axis_names)
    line = np.moveaxis(mesh.devices, names.index("tensor"), 0).reshape(count, -1)[:, 0]
    natural = list(range(count))
    places = [tuple(getattr(device, "coords", ()) or ()) for device in line]
    if not all(len(place) == 3 for place in places):
        return natural
    varying = [d for d in range(3) if len({place[d] for place in places}) > 1]
    if len(varying) != 2:
        return natural
    inner = [d for d in varying if len({place[d] for place in places}) == 2]
    if not inner:
        return natural
    side = inner[-1]
    along = varying[0] if varying[1] == side else varying[1]
    low = min(place[side] for place in places)
    up = sorted((i for i in natural if places[i][side] == low), key=lambda i: places[i][along])
    down = sorted((i for i in natural if places[i][side] != low), key=lambda i: -places[i][along])
    return up + down


def fetch_kernel(*refs):
    count = (len(refs) - 1) // 2
    copies = [pltpu.make_async_copy(refs[i], refs[count + i], refs[-1].at[i]) for i in range(count)]
    for copy in copies:
        copy.start()
    for copy in copies:
        copy.wait()


def fetch(*arrays):
    return pl.pallas_call(
        fetch_kernel,
        out_shape=[pltpu.VMEM(a.shape, a.dtype) for a in arrays],
        in_specs=[pl.BlockSpec(memory_space=pl.ANY)] * len(arrays),
        out_specs=[pl.BlockSpec(memory_space=pltpu.VMEM)] * len(arrays),
        scratch_shapes=[pltpu.SemaphoreType.DMA((len(arrays),))],
        compiler_params=pltpu.CompilerParams(vmem_limit_bytes=4 * 1024 * 1024),
    )(*[pltpu.with_memory_space_constraint(a, pltpu.HBM) for a in arrays])


def route_kernel(own, ids, gates, tokens, mine, theirs, coefficient):
    rows_here, capacity = tokens.shape[0], mine.shape[0]
    place = lax.broadcasted_iota(jnp.int32, (2 * capacity, rows_here), 0)
    expert = jnp.where(place < capacity, own[0], 1 - own[0])
    slots = jnp.where(place < capacity, place, place - capacity).astype(jnp.float32)
    earlier = lax.broadcasted_iota(jnp.int32, (rows_here, rows_here), 0) < lax.broadcasted_iota(
        jnp.int32, (rows_here, rows_here), 1
    )
    matches = [ids[k : k + 1, :] == expert for k in range(ids.shape[0])]
    picked = functools.reduce(jnp.logical_or, matches)
    weight = sum(jnp.where(match, gates[k : k + 1, :], 0.0) for k, match in enumerate(matches))
    slot = jnp.dot(
        picked.astype(jnp.float32).astype(jnp.bfloat16),
        earlier.astype(jnp.float32).astype(jnp.bfloat16),
        preferred_element_type=jnp.float32,
    )
    onehot = jnp.where(picked & (slot == slots), 1.0, 0.0)
    rows = jnp.dot(onehot.astype(jnp.bfloat16), tokens[...], preferred_element_type=jnp.float32)
    mine[...] = rows[:capacity].astype(mine.dtype)
    theirs[...] = rows[capacity:].astype(theirs.dtype)
    coefficient[...] = onehot * weight


def route(own, ids, gates, tokens):
    rows_here, width = tokens.shape
    capacity = rows_here // 4
    in_vmem = pl.BlockSpec(memory_space=pltpu.VMEM)
    return pl.pallas_call(
        route_kernel,
        out_shape=[
            pltpu.VMEM((capacity, width), tokens.dtype),
            pltpu.VMEM((capacity, width), tokens.dtype),
            pltpu.VMEM((2 * capacity, rows_here), jnp.float32),
        ],
        in_specs=[pl.BlockSpec(memory_space=pltpu.SMEM)] + [in_vmem] * 3,
        out_specs=[in_vmem] * 3,
        compiler_params=pltpu.CompilerParams(vmem_limit_bytes=4 * 1024 * 1024),
        cost_estimate=pl.CostEstimate(flops=30_000_000_000, bytes_accessed=0, transcendentals=0),
    )(own, *[pltpu.with_memory_space_constraint(a, pltpu.VMEM) for a in fetch(ids, gates, tokens)])


def presum_kernel(counts, *refs):
    parts, outs = refs[:-2], refs[-2:]
    for group, out in zip((parts[: counts[0]], parts[counts[0] :]), outs):
        total = group[0][...].astype(jnp.float32)
        for part in group[1:]:
            total = total + part[...].astype(jnp.float32)
        out[...] = total


def presum(own, other):
    in_vmem = pl.BlockSpec(memory_space=pltpu.VMEM)
    parts = [pltpu.with_memory_space_constraint(part, pltpu.VMEM) for part in (*own, *other)]
    return pl.pallas_call(
        functools.partial(presum_kernel, (len(own), len(other))),
        out_shape=[pltpu.VMEM(own[0].shape, jnp.float32)] * 2,
        in_specs=[in_vmem] * len(parts),
        out_specs=[in_vmem] * 2,
        compiler_params=pltpu.CompilerParams(vmem_limit_bytes=4 * 1024 * 1024),
        cost_estimate=pl.CostEstimate(flops=4_000_000_000, bytes_accessed=0, transcendentals=0),
    )(*parts)


def combine_kernel(counts, coefficient, *refs):
    (*parts, out) = refs
    left = coefficient[...]
    high = left.astype(jnp.bfloat16)
    rest = left - high.astype(jnp.float32)
    middle = rest.astype(jnp.bfloat16)
    low = (rest - middle.astype(jnp.float32)).astype(jnp.bfloat16)
    split = jnp.concatenate([high, middle, low], axis=0)
    sums = []
    for group in (parts[: counts[0]], parts[counts[0] :]):
        total = group[0][...].astype(jnp.float32)
        for part in group[1:]:
            total = total + part[...].astype(jnp.float32)
        sums.append(total.astype(jnp.bfloat16))
    pair = jnp.concatenate(sums, axis=0)
    rows = jnp.concatenate([pair, pair, pair], axis=0)
    out[...] = lax.dot_general(
        split, rows, (((0,), (0,)), ((), ())), preferred_element_type=jnp.float32
    ).astype(out.dtype)


def combine(coefficient, own, other):
    rows_here, width = coefficient.shape[1], own[0].shape[1]
    in_vmem = pl.BlockSpec(memory_space=pltpu.VMEM)
    parts = [pltpu.with_memory_space_constraint(part, pltpu.VMEM) for part in (*own, *other)]
    return pl.pallas_call(
        functools.partial(combine_kernel, (len(own), len(other))),
        out_shape=jax.ShapeDtypeStruct((rows_here, width), jnp.bfloat16),
        in_specs=[in_vmem] * (1 + len(parts)),
        out_specs=in_vmem,
        compiler_params=pltpu.CompilerParams(vmem_limit_bytes=6 * 1024 * 1024),
    )(coefficient, *parts)


def feed_forward_kernel(count, capacity, *refs):
    blocks, (w_gate, w_up, w_down) = refs[:count], refs[count : count + 3]
    outs = refs[count + 3 : 2 * count + 3]
    rows, gate, hidden, parts = refs[2 * count + 3 :]
    for i, block in enumerate(blocks):
        rows[i * capacity : (i + 1) * capacity, :] = block[...]
    gate[...] = jnp.dot(rows[...], w_gate[...], preferred_element_type=jnp.float32)
    up = jnp.dot(rows[...], w_up[...], preferred_element_type=jnp.float32)
    hidden[...] = (gate[...] / (1.0 + jnp.exp(-gate[...])) * up).astype(hidden.dtype)
    parts[...] = jnp.dot(hidden[...], w_down[...], preferred_element_type=jnp.float32).astype(parts.dtype)
    for i, out in enumerate(outs):
        out[...] = parts[i * capacity : (i + 1) * capacity, :].astype(out.dtype)


def feed_forward(blocks, w_gate, w_up, w_down):
    count, (capacity, width) = len(blocks), blocks[0].shape
    units = w_down.shape[0]
    weights = [pltpu.with_memory_space_constraint(w, pltpu.VMEM) for w in (w_gate, w_up, w_down)]
    in_vmem = pl.BlockSpec(memory_space=pltpu.VMEM)
    parts = pl.pallas_call(
        functools.partial(feed_forward_kernel, count, capacity),
        out_shape=[pltpu.VMEM((capacity, width), jnp.float32) for _ in blocks],
        in_specs=[in_vmem] * (count + 3),
        out_specs=[in_vmem] * count,
        scratch_shapes=[
            pltpu.VMEM((count * capacity, width), jnp.bfloat16),
            pltpu.VMEM((count * capacity, units), jnp.float32),
            pltpu.VMEM((count * capacity, units), jnp.bfloat16),
            pltpu.VMEM((count * capacity, width), jnp.float32),
        ],
        compiler_params=pltpu.CompilerParams(vmem_limit_bytes=12 * 1024 * 1024),
        cost_estimate=pl.CostEstimate(
            flops=6 * count * capacity * width * units, bytes_accessed=0, transcendentals=0
        ),
    )(*[pltpu.with_memory_space_constraint(b, pltpu.VMEM) for b in blocks], *weights)
    return parts


def make_per_device(ring):
    count = len(ring)
    near, opposite = (count - 1) // 2, count // 2
    swap = [(0, 1), (1, 0)]
    long = (1, -1)
    steps = [(chain, -way * step, way) for step in range(1, near + 1) for chain in (0, 1) for way in (1, -1)]
    if count % 2 == 0:
        steps += [(chain, -long[chain] * opposite, long[chain]) for chain in (0, 1)]

    def send(block, hops, crossing=False):
        perm = [
            (2 * ring[i] + core, 2 * ring[(i + hops) % count] + (1 - core if crossing else core))
            for i in range(count)
            for core in (0, 1)
        ]
        return lax.ppermute(block, ("tensor", "expert"), perm)

    def gather(mine, theirs):
        held = ({0: mine}, {0: lax.ppermute(theirs, "expert", swap)})
        for chain, place, way in steps:
            if abs(place) == opposite and near and count % 2 == 0:
                held[chain][place] = send(held[chain][place + 2 * way], 2 * way)
            elif place + way:
                held[chain][place] = send(held[chain][place + way], way)
            else:
                held[chain][place] = send(theirs if chain else mine, way, crossing=chain == 1)
        return held

    def scatter(terms):
        arrived, early, last = {}, ([], []), [None, None]
        for chain, place, way in reversed(steps):
            term = terms[chain][place if abs(place) == opposite and count % 2 == 0 else -place].astype(jnp.float32)
            if (chain, place, way) in arrived:
                term = term + arrived[chain, place, way].astype(jnp.float32)
            got = send(term.astype(jnp.bfloat16), way, crossing=chain == 1 and place + way == 0)
            if place + way:
                arrived[chain, place + way, way] = got
            elif way == long[chain]:
                last[chain] = got
            else:
                early[chain].append(got)
        other = lax.ppermute(terms[1][0].astype(jnp.bfloat16), "expert", swap)
        return presum([terms[0][0], *early[0]], [other, *early[1]]), last

    def per_device(tokens, expert_ids, gates, w_gate, w_up, w_down):
        own = lax.axis_index("expert").astype(jnp.int32).reshape(1)
        mine, theirs, coefficient = route(own, expert_ids.T, gates.T, tokens)
        held = gather(mine, theirs)
        places = [(chain, place) for chain in (0, 1) for place in held[chain]]
        parts = feed_forward([held[c][p] for c, p in places], w_gate[0], w_up[0], w_down[0])
        terms = ({}, {})
        for (chain, place), part in zip(places, parts):
            terms[chain][place] = part
        sums, last = scatter(terms)
        own, other = ([first] if late is None else [first, late] for first, late in zip(sums, last))
        return combine(coefficient, own, other)

    return per_device


def solution(mesh):
    placed = (
        P(("groups", "tensor", "expert"), None),
        P(("groups", "tensor", "expert"), None),
        P(("groups", "tensor", "expert"), None),
        P("expert", None, "tensor"),
        P("expert", None, "tensor"),
        P("expert", "tensor", None),
    )
    return jax.shard_map(
        make_per_device(ring_order(mesh)),
        mesh=mesh,
        in_specs=placed,
        out_specs=P(("groups", "tensor", "expert"), None),
        check_vma=False,
    )
```

```python
import functools

import jax
import jax.numpy as jnp
import numpy as np
from jax import lax
from jax.experimental import pallas as pl
from jax.experimental.pallas import tpu as pltpu
from jax.sharding import PartitionSpec as P


def ring_order(mesh):
    count = mesh.shape["tensor"]
    names = list(mesh.axis_names)
    line = np.moveaxis(mesh.devices, names.index("tensor"), 0).reshape(count, -1)[:, 0]
    natural = list(range(count))
    places = [tuple(getattr(device, "coords", ()) or ()) for device in line]
    if not all(len(place) == 3 for place in places):
        return natural
    varying = [d for d in range(3) if len({place[d] for place in places}) > 1]
    if len(varying) != 2:
        return natural
    inner = [d for d in varying if len({place[d] for place in places}) == 2]
    if not inner:
        return natural
    side = inner[-1]
    along = varying[0] if varying[1] == side else varying[1]
    low = min(place[side] for place in places)
    up = sorted((i for i in natural if places[i][side] == low), key=lambda i: places[i][along])
    down = sorted((i for i in natural if places[i][side] != low), key=lambda i: -places[i][along])
    return up + down


def fetch_kernel(*refs):
    count = (len(refs) - 1) // 2
    copies = [pltpu.make_async_copy(refs[i], refs[count + i], refs[-1].at[i]) for i in range(count)]
    for copy in copies:
        copy.start()
    for copy in copies:
        copy.wait()


def fetch(*arrays):
    return pl.pallas_call(
        fetch_kernel,
        out_shape=[pltpu.VMEM(a.shape, a.dtype) for a in arrays],
        in_specs=[pl.BlockSpec(memory_space=pl.ANY)] * len(arrays),
        out_specs=[pl.BlockSpec(memory_space=pltpu.VMEM)] * len(arrays),
        scratch_shapes=[pltpu.SemaphoreType.DMA((len(arrays),))],
        compiler_params=pltpu.CompilerParams(vmem_limit_bytes=4 * 1024 * 1024),
    )(*[pltpu.with_memory_space_constraint(a, pltpu.HBM) for a in arrays])


def route_kernel(own, ids, gates, tokens, mine, theirs, coefficient):
    rows_here, capacity = tokens.shape[0], mine.shape[0]
    place = lax.broadcasted_iota(jnp.int32, (2 * capacity, rows_here), 0)
    expert = jnp.where(place < capacity, own[0], 1 - own[0])
    slots = jnp.where(place < capacity, place, place - capacity).astype(jnp.float32)
    earlier = lax.broadcasted_iota(jnp.int32, (rows_here, rows_here), 0) < lax.broadcasted_iota(
        jnp.int32, (rows_here, rows_here), 1
    )
    matches = [ids[k : k + 1, :] == expert for k in range(ids.shape[0])]
    picked = functools.reduce(jnp.logical_or, matches)
    weight = sum(jnp.where(match, gates[k : k + 1, :], 0.0) for k, match in enumerate(matches))
    slot = jnp.dot(
        picked.astype(jnp.float32).astype(jnp.bfloat16),
        earlier.astype(jnp.float32).astype(jnp.bfloat16),
        preferred_element_type=jnp.float32,
    )
    onehot = jnp.where(picked & (slot == slots), 1.0, 0.0)
    rows = jnp.dot(onehot.astype(jnp.bfloat16), tokens[...], preferred_element_type=jnp.float32)
    mine[...] = rows[:capacity].astype(mine.dtype)
    theirs[...] = rows[capacity:].astype(theirs.dtype)
    coefficient[...] = onehot * weight


def route(own, ids, gates, tokens):
    rows_here, width = tokens.shape
    capacity = rows_here // 4
    in_vmem = pl.BlockSpec(memory_space=pltpu.VMEM)
    return pl.pallas_call(
        route_kernel,
        out_shape=[
            pltpu.VMEM((capacity, width), tokens.dtype),
            pltpu.VMEM((capacity, width), tokens.dtype),
            pltpu.VMEM((2 * capacity, rows_here), jnp.float32),
        ],
        in_specs=[pl.BlockSpec(memory_space=pltpu.SMEM)] + [in_vmem] * 3,
        out_specs=[in_vmem] * 3,
        compiler_params=pltpu.CompilerParams(vmem_limit_bytes=4 * 1024 * 1024),
        cost_estimate=pl.CostEstimate(flops=30_000_000_000, bytes_accessed=0, transcendentals=0),
    )(own, *[pltpu.with_memory_space_constraint(a, pltpu.VMEM) for a in fetch(ids, gates, tokens)])


def presum_kernel(counts, *refs):
    parts, outs = refs[:-2], refs[-2:]
    for group, out in zip((parts[: counts[0]], parts[counts[0] :]), outs):
        total = group[0][...].astype(jnp.float32)
        for part in group[1:]:
            total = total + part[...].astype(jnp.float32)
        out[...] = total


def presum(own, other):
    in_vmem = pl.BlockSpec(memory_space=pltpu.VMEM)
    parts = [pltpu.with_memory_space_constraint(part, pltpu.VMEM) for part in (*own, *other)]
    return pl.pallas_call(
        functools.partial(presum_kernel, (len(own), len(other))),
        out_shape=[pltpu.VMEM(own[0].shape, jnp.float32)] * 2,
        in_specs=[in_vmem] * len(parts),
        out_specs=[in_vmem] * 2,
        compiler_params=pltpu.CompilerParams(vmem_limit_bytes=4 * 1024 * 1024),
        cost_estimate=pl.CostEstimate(flops=4_000_000_000, bytes_accessed=0, transcendentals=0),
    )(*parts)


def combine_kernel(counts, coefficient, *refs):
    (*parts, out) = refs
    left = coefficient[...]
    high = left.astype(jnp.bfloat16)
    rest = left - high.astype(jnp.float32)
    middle = rest.astype(jnp.bfloat16)
    low = (rest - middle.astype(jnp.float32)).astype(jnp.bfloat16)
    split = jnp.concatenate([high, middle, low], axis=0)
    sums = []
    for group in (parts[: counts[0]], parts[counts[0] :]):
        total = group[0][...].astype(jnp.float32)
        for part in group[1:]:
            total = total + part[...].astype(jnp.float32)
        sums.append(total.astype(jnp.bfloat16))
    pair = jnp.concatenate(sums, axis=0)
    rows = jnp.concatenate([pair, pair, pair], axis=0)
    out[...] = lax.dot_general(
        split, rows, (((0,), (0,)), ((), ())), preferred_element_type=jnp.float32
    ).astype(out.dtype)


def combine(coefficient, own, other):
    rows_here, width = coefficient.shape[1], own[0].shape[1]
    in_vmem = pl.BlockSpec(memory_space=pltpu.VMEM)
    parts = [pltpu.with_memory_space_constraint(part, pltpu.VMEM) for part in (*own, *other)]
    return pl.pallas_call(
        functools.partial(combine_kernel, (len(own), len(other))),
        out_shape=jax.ShapeDtypeStruct((rows_here, width), jnp.bfloat16),
        in_specs=[in_vmem] * (1 + len(parts)),
        out_specs=in_vmem,
        compiler_params=pltpu.CompilerParams(vmem_limit_bytes=6 * 1024 * 1024),
    )(coefficient, *parts)


def feed_forward_kernel(count, capacity, *refs):
    blocks, (w_gate, w_up, w_down) = refs[:count], refs[count : count + 3]
    outs = refs[count + 3 : 2 * count + 3]
    rows, gate, hidden, parts = refs[2 * count + 3 :]
    for i, block in enumerate(blocks):
        rows[i * capacity : (i + 1) * capacity, :] = block[...]
    gate[...] = jnp.dot(rows[...], w_gate[...], preferred_element_type=jnp.float32)
    up = jnp.dot(rows[...], w_up[...], preferred_element_type=jnp.float32)
    hidden[...] = (gate[...] / (1.0 + jnp.exp(-gate[...])) * up).astype(hidden.dtype)
    parts[...] = jnp.dot(hidden[...], w_down[...], preferred_element_type=jnp.float32).astype(parts.dtype)
    for i, out in enumerate(outs):
        out[...] = parts[i * capacity : (i + 1) * capacity, :].astype(out.dtype)


def feed_forward(blocks, w_gate, w_up, w_down):
    count, (capacity, width) = len(blocks), blocks[0].shape
    units = w_down.shape[0]
    weights = [pltpu.with_memory_space_constraint(w, pltpu.VMEM) for w in (w_gate, w_up, w_down)]
    in_vmem = pl.BlockSpec(memory_space=pltpu.VMEM)
    parts = pl.pallas_call(
        functools.partial(feed_forward_kernel, count, capacity),
        out_shape=[pltpu.VMEM((capacity, width), jnp.float32) for _ in blocks],
        in_specs=[in_vmem] * (count + 3),
        out_specs=[in_vmem] * count,
        scratch_shapes=[
            pltpu.VMEM((count * capacity, width), jnp.bfloat16),
            pltpu.VMEM((count * capacity, units), jnp.float32),
            pltpu.VMEM((count * capacity, units), jnp.bfloat16),
            pltpu.VMEM((count * capacity, width), jnp.float32),
        ],
        compiler_params=pltpu.CompilerParams(vmem_limit_bytes=12 * 1024 * 1024),
        cost_estimate=pl.CostEstimate(
            flops=6 * count * capacity * width * units, bytes_accessed=0, transcendentals=0
        ),
    )(*[pltpu.with_memory_space_constraint(b, pltpu.VMEM) for b in blocks], *weights)
    return parts


def make_per_device(ring):
    count = len(ring)
    near, opposite = (count - 1) // 2, count // 2
    swap = [(0, 1), (1, 0)]
    def outwards(long):
        steps = [(chain, -way * step, way) for step in range(1, near + 1) for way in (1, -1) for chain in (0, 1)]
        if count % 2 == 0:
            steps += [(chain, -long[chain] * opposite, long[chain]) for chain in (0, 1)]
        return steps

    def send(block, hops, crossing=False):
        perm = [
            (2 * ring[i] + core, 2 * ring[(i + hops) % count] + (1 - core if crossing else core))
            for i in range(count)
            for core in (0, 1)
        ]
        return lax.ppermute(block, ("tensor", "expert"), perm)

    def gather(mine, theirs):
        held = ({0: mine}, {0: lax.ppermute(theirs, "expert", swap)})
        for chain, place, way in outwards((1, -1)):
            if abs(place) == opposite and near and count % 2 == 0:
                held[chain][place] = send(held[chain][place + 2 * way], 2 * way)
            elif place + way:
                held[chain][place] = send(held[chain][place + way], way)
            else:
                held[chain][place] = send(theirs if chain else mine, way, crossing=chain == 1)
        return held

    def scatter(terms):
        long = (-1, 1)
        arrived, early, last = {}, ([], []), [None, None]
        for chain, place, way in reversed(outwards(long)):
            term = terms[chain][-place if -place in terms[chain] else place].astype(jnp.float32)
            if (chain, place, way) in arrived:
                term = term + arrived[chain, place, way].astype(jnp.float32)
            got = send(term.astype(jnp.bfloat16), way, crossing=chain == 1 and place + way == 0)
            if place + way:
                arrived[chain, place + way, way] = got
            elif way == long[chain]:
                last[chain] = got
            else:
                early[chain].append(got)
        other = lax.ppermute(terms[1][0].astype(jnp.bfloat16), "expert", swap)
        return presum([terms[0][0], *early[0]], [other, *early[1]]), last

    def per_device(tokens, expert_ids, gates, w_gate, w_up, w_down):
        own = lax.axis_index("expert").astype(jnp.int32).reshape(1)
        mine, theirs, coefficient = route(own, expert_ids.T, gates.T, tokens)
        held = gather(mine, theirs)
        places = [(chain, place) for chain in (0, 1) for place in held[chain]]
        parts = feed_forward([held[c][p] for c, p in places], w_gate[0], w_up[0], w_down[0])
        terms = ({}, {})
        for (chain, place), part in zip(places, parts):
            terms[chain][place] = part
        sums, last = scatter(terms)
        own, other = ([first] if late is None else [first, late] for first, late in zip(sums, last))
        return combine(coefficient, own, other)

    return per_device


def solution(mesh):
    placed = (
        P(("groups", "tensor", "expert"), None),
        P(("groups", "tensor", "expert"), None),
        P(("groups", "tensor", "expert"), None),
        P("expert", None, "tensor"),
        P("expert", None, "tensor"),
        P("expert", "tensor", None),
    )
    return jax.shard_map(
        make_per_device(ring_order(mesh)),
        mesh=mesh,
        in_specs=placed,
        out_specs=P(("groups", "tensor", "expert"), None),
        check_vma=False,
    )
```

```python
import functools

import jax
import jax.numpy as jnp
import numpy as np
from jax import lax
from jax.experimental import pallas as pl
from jax.experimental.pallas import tpu as pltpu
from jax.sharding import PartitionSpec as P


def ring_order(mesh):
    count = mesh.shape["tensor"]
    names = list(mesh.axis_names)
    line = np.moveaxis(mesh.devices, names.index("tensor"), 0).reshape(count, -1)[:, 0]
    natural = list(range(count))
    places = [tuple(getattr(device, "coords", ()) or ()) for device in line]
    if not all(len(place) == 3 for place in places):
        return natural
    varying = [d for d in range(3) if len({place[d] for place in places}) > 1]
    if len(varying) != 2:
        return natural
    inner = [d for d in varying if len({place[d] for place in places}) == 2]
    if not inner:
        return natural
    side = inner[-1]
    along = varying[0] if varying[1] == side else varying[1]
    low = min(place[side] for place in places)
    up = sorted((i for i in natural if places[i][side] == low), key=lambda i: places[i][along])
    down = sorted((i for i in natural if places[i][side] != low), key=lambda i: -places[i][along])
    return up + down


def fetch_kernel(*refs):
    count = (len(refs) - 1) // 2
    copies = [pltpu.make_async_copy(refs[i], refs[count + i], refs[-1].at[i]) for i in range(count)]
    for copy in copies:
        copy.start()
    for copy in copies:
        copy.wait()


def fetch(*arrays):
    return pl.pallas_call(
        fetch_kernel,
        out_shape=[pltpu.VMEM(a.shape, a.dtype) for a in arrays],
        in_specs=[pl.BlockSpec(memory_space=pl.ANY)] * len(arrays),
        out_specs=[pl.BlockSpec(memory_space=pltpu.VMEM)] * len(arrays),
        scratch_shapes=[pltpu.SemaphoreType.DMA((len(arrays),))],
        compiler_params=pltpu.CompilerParams(vmem_limit_bytes=4 * 1024 * 1024),
    )(*[pltpu.with_memory_space_constraint(a, pltpu.HBM) for a in arrays])


def route_kernel(own, ids, gates, tokens, mine, theirs, coefficient):
    rows_here, capacity = tokens.shape[0], mine.shape[0]
    place = lax.broadcasted_iota(jnp.int32, (2 * capacity, rows_here), 0)
    expert = jnp.where(place < capacity, own[0], 1 - own[0])
    slots = jnp.where(place < capacity, place, place - capacity).astype(jnp.float32)
    earlier = lax.broadcasted_iota(jnp.int32, (rows_here, rows_here), 0) < lax.broadcasted_iota(
        jnp.int32, (rows_here, rows_here), 1
    )
    matches = [ids[k : k + 1, :] == expert for k in range(ids.shape[0])]
    picked = functools.reduce(jnp.logical_or, matches)
    weight = sum(jnp.where(match, gates[k : k + 1, :], 0.0) for k, match in enumerate(matches))
    slot = jnp.dot(
        picked.astype(jnp.float32).astype(jnp.bfloat16),
        earlier.astype(jnp.float32).astype(jnp.bfloat16),
        preferred_element_type=jnp.float32,
    )
    onehot = jnp.where(picked & (slot == slots), 1.0, 0.0)
    rows = jnp.dot(onehot.astype(jnp.bfloat16), tokens[...], preferred_element_type=jnp.float32)
    mine[...] = rows[:capacity].astype(mine.dtype)
    theirs[...] = rows[capacity:].astype(theirs.dtype)
    coefficient[...] = onehot * weight


def route(own, ids, gates, tokens):
    rows_here, width = tokens.shape
    capacity = rows_here // 4
    in_vmem = pl.BlockSpec(memory_space=pltpu.VMEM)
    return pl.pallas_call(
        route_kernel,
        out_shape=[
            pltpu.VMEM((capacity, width), tokens.dtype),
            pltpu.VMEM((capacity, width), tokens.dtype),
            pltpu.VMEM((2 * capacity, rows_here), jnp.float32),
        ],
        in_specs=[pl.BlockSpec(memory_space=pltpu.SMEM)] + [in_vmem] * 3,
        out_specs=[in_vmem] * 3,
        compiler_params=pltpu.CompilerParams(vmem_limit_bytes=4 * 1024 * 1024),
        cost_estimate=pl.CostEstimate(flops=30_000_000_000, bytes_accessed=0, transcendentals=0),
    )(own, *[pltpu.with_memory_space_constraint(a, pltpu.VMEM) for a in fetch(ids, gates, tokens)])


def presum_kernel(counts, *refs):
    parts, outs = refs[:-2], refs[-2:]
    for group, out in zip((parts[: counts[0]], parts[counts[0] :]), outs):
        total = group[0][...].astype(jnp.float32)
        for part in group[1:]:
            total = total + part[...].astype(jnp.float32)
        out[...] = total


def presum(own, other):
    in_vmem = pl.BlockSpec(memory_space=pltpu.VMEM)
    parts = [pltpu.with_memory_space_constraint(part, pltpu.VMEM) for part in (*own, *other)]
    return pl.pallas_call(
        functools.partial(presum_kernel, (len(own), len(other))),
        out_shape=[pltpu.VMEM(own[0].shape, jnp.float32)] * 2,
        in_specs=[in_vmem] * len(parts),
        out_specs=[in_vmem] * 2,
        compiler_params=pltpu.CompilerParams(vmem_limit_bytes=4 * 1024 * 1024),
        cost_estimate=pl.CostEstimate(flops=9_000_000_000, bytes_accessed=0, transcendentals=0),
    )(*parts)


def combine_kernel(counts, coefficient, *refs):
    (*parts, out) = refs
    left = coefficient[...]
    high = left.astype(jnp.bfloat16)
    rest = left - high.astype(jnp.float32)
    middle = rest.astype(jnp.bfloat16)
    low = (rest - middle.astype(jnp.float32)).astype(jnp.bfloat16)
    split = jnp.concatenate([high, middle, low], axis=0)
    sums = []
    for group in (parts[: counts[0]], parts[counts[0] :]):
        total = group[0][...].astype(jnp.float32)
        for part in group[1:]:
            total = total + part[...].astype(jnp.float32)
        sums.append(total.astype(jnp.bfloat16))
    pair = jnp.concatenate(sums, axis=0)
    rows = jnp.concatenate([pair, pair, pair], axis=0)
    out[...] = lax.dot_general(
        split, rows, (((0,), (0,)), ((), ())), preferred_element_type=jnp.float32
    ).astype(out.dtype)


def combine(coefficient, own, other):
    rows_here, width = coefficient.shape[1], own[0].shape[1]
    in_vmem = pl.BlockSpec(memory_space=pltpu.VMEM)
    parts = [pltpu.with_memory_space_constraint(part, pltpu.VMEM) for part in (*own, *other)]
    return pl.pallas_call(
        functools.partial(combine_kernel, (len(own), len(other))),
        out_shape=jax.ShapeDtypeStruct((rows_here, width), jnp.bfloat16),
        in_specs=[in_vmem] * (1 + len(parts)),
        out_specs=in_vmem,
        compiler_params=pltpu.CompilerParams(vmem_limit_bytes=6 * 1024 * 1024),
    )(coefficient, *parts)


def feed_forward_kernel(count, capacity, *refs):
    blocks, (w_gate, w_up, w_down) = refs[:count], refs[count : count + 3]
    outs = refs[count + 3 : 2 * count + 3]
    rows, gate, hidden, parts = refs[2 * count + 3 :]
    for i, block in enumerate(blocks):
        rows[i * capacity : (i + 1) * capacity, :] = block[...]
    gate[...] = jnp.dot(rows[...], w_gate[...], preferred_element_type=jnp.float32)
    up = jnp.dot(rows[...], w_up[...], preferred_element_type=jnp.float32)
    hidden[...] = (gate[...] / (1.0 + jnp.exp(-gate[...])) * up).astype(hidden.dtype)
    parts[...] = jnp.dot(hidden[...], w_down[...], preferred_element_type=jnp.float32).astype(parts.dtype)
    for i, out in enumerate(outs):
        out[...] = parts[i * capacity : (i + 1) * capacity, :].astype(out.dtype)


def feed_forward(blocks, w_gate, w_up, w_down):
    count, (capacity, width) = len(blocks), blocks[0].shape
    units = w_down.shape[0]
    weights = [pltpu.with_memory_space_constraint(w, pltpu.VMEM) for w in (w_gate, w_up, w_down)]
    in_vmem = pl.BlockSpec(memory_space=pltpu.VMEM)
    parts = pl.pallas_call(
        functools.partial(feed_forward_kernel, count, capacity),
        out_shape=[pltpu.VMEM((capacity, width), jnp.float32) for _ in blocks],
        in_specs=[in_vmem] * (count + 3),
        out_specs=[in_vmem] * count,
        scratch_shapes=[
            pltpu.VMEM((count * capacity, width), jnp.bfloat16),
            pltpu.VMEM((count * capacity, units), jnp.float32),
            pltpu.VMEM((count * capacity, units), jnp.bfloat16),
            pltpu.VMEM((count * capacity, width), jnp.float32),
        ],
        compiler_params=pltpu.CompilerParams(vmem_limit_bytes=12 * 1024 * 1024),
        cost_estimate=pl.CostEstimate(
            flops=6 * count * capacity * width * units, bytes_accessed=0, transcendentals=0
        ),
    )(*[pltpu.with_memory_space_constraint(b, pltpu.VMEM) for b in blocks], *weights)
    return parts


def make_per_device(ring):
    count = len(ring)
    near, opposite = (count - 1) // 2, count // 2
    swap = [(0, 1), (1, 0)]
    def outwards(long):
        steps = [(chain, -way * step, way) for step in range(1, near + 1) for way in (1, -1) for chain in (0, 1)]
        if count % 2 == 0:
            steps += [(chain, -long[chain] * opposite, long[chain]) for chain in (0, 1)]
        return steps

    def send(block, hops, crossing=False):
        perm = [
            (2 * ring[i] + core, 2 * ring[(i + hops) % count] + (1 - core if crossing else core))
            for i in range(count)
            for core in (0, 1)
        ]
        return lax.ppermute(block, ("tensor", "expert"), perm)

    def gather(mine, theirs):
        held = ({0: mine}, {0: lax.ppermute(theirs, "expert", swap)})
        for chain, place, way in outwards((1, -1)):
            if abs(place) == opposite and near and count % 2 == 0:
                held[chain][place] = send(held[chain][place + 2 * way], 2 * way)
            elif place + way:
                held[chain][place] = send(held[chain][place + way], way)
            else:
                held[chain][place] = send(theirs if chain else mine, way, crossing=chain == 1)
        return held

    def scatter(terms):
        long = (-1, 1)
        arrived, early, last = {}, ([], []), [None, None]
        for chain, place, way in reversed(outwards(long)):
            term = terms[chain][-place if -place in terms[chain] else place].astype(jnp.float32)
            if (chain, place, way) in arrived:
                term = term + arrived[chain, place, way].astype(jnp.float32)
            got = send(term.astype(jnp.bfloat16), way, crossing=chain == 1 and place + way == 0)
            if place + way:
                arrived[chain, place + way, way] = got
            elif way == long[chain]:
                last[chain] = got
            else:
                early[chain].append(got)
        other = lax.ppermute(terms[1][0].astype(jnp.bfloat16), "expert", swap)
        return presum([terms[0][0], *early[0]], [other, *early[1]]), last

    def per_device(tokens, expert_ids, gates, w_gate, w_up, w_down):
        own = lax.axis_index("expert").astype(jnp.int32).reshape(1)
        mine, theirs, coefficient = route(own, expert_ids.T, gates.T, tokens)
        held = gather(mine, theirs)
        places = [(chain, place) for chain in (0, 1) for place in held[chain]]
        parts = feed_forward([held[c][p] for c, p in places], w_gate[0], w_up[0], w_down[0])
        terms = ({}, {})
        for (chain, place), part in zip(places, parts):
            terms[chain][place] = part
        sums, last = scatter(terms)
        own, other = ([first] if late is None else [first, late] for first, late in zip(sums, last))
        return combine(coefficient, own, other)

    return per_device


def solution(mesh):
    placed = (
        P(("groups", "tensor", "expert"), None),
        P(("groups", "tensor", "expert"), None),
        P(("groups", "tensor", "expert"), None),
        P("expert", None, "tensor"),
        P("expert", None, "tensor"),
        P("expert", "tensor", None),
    )
    return jax.shard_map(
        make_per_device(ring_order(mesh)),
        mesh=mesh,
        in_specs=placed,
        out_specs=P(("groups", "tensor", "expert"), None),
        check_vma=False,
    )
```
